32 devices in a mesh: fsdp: 4 (over z), heads: 2 (over core), tensor: 4 (over y, x).
Axes of the slice: x: 2, y: 2, z: 4, core: 2. Of those that a mesh axis runs over, the one named last changes fastest.
Arguments:
- tokens: bfloat16 [16, 1024, 1152], P(('fsdp', 'tensor'), 'heads'), may hold values from -6 to 6
- seq_lens: int32 [16, 8], P(('fsdp', 'tensor')), may hold values from 0 to 1024, as said below
- cotangent: bfloat16 [16, 1024, 1152], P(('fsdp', 'tensor'), 'heads'), may hold values from -6 to 6
- w_query: bfloat16 [1152, 1152], P(('fsdp', 'tensor'), 'heads'), may hold values from -0.1875 to 0.1875
- w_key: bfloat16 [1152, 384], P(('fsdp', 'tensor'), 'heads'), may hold values from -0.1875 to 0.1875
- w_value: bfloat16 [1152, 384], P(('fsdp', 'tensor'), 'heads'), may hold values from -0.1875 to 0.1875
- w_out: bfloat16 [1152, 1152], P('heads', ('fsdp', 'tensor')), may hold values from -1.5 to 1.5
- norm_first: bfloat16 [1152], P(('fsdp', 'tensor')), may hold values from 0.5 to 1.5
- norm_second: bfloat16 [1152], P(('fsdp', 'tensor')), may hold values from 0.5 to 1.5
- w_gate: bfloat16 [1152, 3072], P(('fsdp', 'heads'), 'tensor'), may hold values from -0.1875 to 0.1875
- w_up: bfloat16 [1152, 3072], P(('fsdp', 'heads'), 'tensor'), may hold values from -0.1875 to 0.1875
- w_down: bfloat16 [3072, 1152], P('tensor', ('fsdp', 'heads')), may hold values from -0.109375 to 0.109375
Outputs:
- layer_out: bfloat16 [16, 1024, 1152], P(('fsdp', 'tensor'), 'heads')
- grad_tokens: float32 [16, 1024, 1152], P(('fsdp', 'tensor'), 'heads')
- grad_query: float32 [1152, 1152], P(('fsdp', 'tensor'), 'heads')
- grad_key: float32 [1152, 384], P(('fsdp', 'tensor'), 'heads')
- grad_value: float32 [1152, 384], P(('fsdp', 'tensor'), 'heads')
- grad_out: float32 [1152, 1152], P('heads', ('fsdp', 'tensor'))
- grad_norm_first: float32 [1152], P(('fsdp', 'tensor'))
- grad_norm_second: float32 [1152], P(('fsdp', 'tensor'))
- grad_gate: float32 [1152, 3072], P(('fsdp', 'heads'), 'tensor')
- grad_up: float32 [1152, 3072], P(('fsdp', 'heads'), 'tensor')
- grad_down: float32 [3072, 1152], P('tensor', ('fsdp', 'heads'))
The draws below stay inside these ranges and needn't reach their ends.
Inputs may be any that keep to these rules, and one draw needn't show every extreme that they name: `seq_lens`: each row lists the lengths of up to 8 sequences packed from the block's start, zero for an empty slot; a row sums to at most 1024; in every draw some block holds a single sequence of 1024.
All inputs are finite; a program needn't handle non-finite values.
Results may differ from the reference program's by a relative error of at most 0.02.
Values may be sent and summed in bfloat16 or wider, within the bound.
A program may use at most 128 MiB of HBM per device.

```python
import jax
import jax.numpy as jnp
from jax import lax

D = 1152
HQ = 18
KVH = 6
HD = 64
FF = 3072
SEQ = 1024
SLOTS = 8
BLOCKS = 16


def draw_seq_lens(key, part):
    key = jax.random.fold_in(key, 7)
    limit_key, cut_key, pick_key = jax.random.split(key, 3)
    limits = jax.random.randint(limit_key, (BLOCKS, 1), SEQ // 4, SEQ + 1)
    raw_cuts = jax.random.randint(cut_key, (BLOCKS, SLOTS - 1), 0, SEQ + 1)
    cut_points = jnp.sort(raw_cuts % (limits + 1), axis=1)
    bounds = jnp.concatenate([jnp.zeros((BLOCKS, 1), jnp.int32), cut_points, limits], axis=1)
    lengths = bounds[:, 1:] - bounds[:, :-1]
    full_block = jax.random.randint(pick_key, (), 0, BLOCKS)
    single = jnp.where(jnp.arange(SLOTS) == 0, SEQ, 0)
    lengths = jnp.where((jnp.arange(BLOCKS) == full_block)[:, None], single[None, :], lengths)
    return lengths.astype(jnp.int32)


def shard_levels(own_key, dims, cuts, low, high):
    factor_of, own = 1.0, jax.random.fold_in(own_key, 6)
    for axis_at, blocks in cuts:
        heights = jnp.exp(jax.random.uniform(jax.random.fold_in(own, axis_at), (blocks,), jnp.float32, low / len(cuts), high / len(cuts)))
        factor_of = factor_of * jnp.repeat(heights, dims[axis_at] // blocks).reshape([-1 if axis == axis_at else 1 for axis in range(len(dims))])
    return factor_of


def gaussian(own_key, extent, width, reach, cuts=(), kind=jnp.bfloat16):
    values = jax.random.normal(own_key, extent, jnp.float32) * width
    if len(cuts) > 0:
        values = shard_levels(own_key, extent, cuts, -0.22, 0.18) * values
    return jnp.clip(values, min=-reach, max=reach).astype(kind)


def setup_inputs(seed: int = 0) -> dict:
    key_of = jax.random.split(jax.random.key(seed), 13)
    tokens = gaussian(key_of[0], (BLOCKS, SEQ, D), 1.0, 6.0, ((0, 16), (1, 2)))
    seq_lens = draw_seq_lens(jax.random.fold_in(key_of[12], 71), 0)
    cotangent = gaussian(key_of[2], (BLOCKS, SEQ, D), 1.0, 6.0, ((0, 16), (1, 2)))
    w_query = gaussian(key_of[3], (D, HQ * HD), D ** -0.5, 0.1875, ((0, 16), (1, 2)))
    w_key = gaussian(key_of[4], (D, KVH * HD), D ** -0.5, 0.1875, ((0, 16), (1, 2)))
    w_value = gaussian(key_of[5], (D, KVH * HD), D ** -0.5, 0.1875, ((0, 16), (1, 2)))
    w_out = gaussian(key_of[6], (HQ * HD, D), (HD // 4) ** -0.5, 1.5, ((0, 2), (1, 16)))
    norm_first = jnp.clip(1.0 + 0.1 * jax.random.normal(key_of[7], (D,), jnp.float32), 0.5, 1.5).astype(jnp.bfloat16)
    norm_second = jnp.clip(1.0 + 0.1 * jax.random.normal(key_of[8], (D,), jnp.float32), 0.5, 1.5).astype(jnp.bfloat16)
    w_gate = gaussian(key_of[9], (D, FF), D ** -0.5, 0.1875, ((0, 8), (1, 4)))
    w_up = gaussian(key_of[10], (D, FF), D ** -0.5, 0.1875, ((0, 8), (1, 4)))
    w_down = gaussian(key_of[11], (FF, D), FF ** -0.5, 0.109375, ((0, 4), (1, 8)))
    return dict(tokens=tokens, seq_lens=seq_lens, cotangent=cotangent, w_query=w_query, w_key=w_key, w_value=w_value, w_out=w_out, norm_first=norm_first, norm_second=norm_second, w_gate=w_gate, w_up=w_up, w_down=w_down)


epsilon = 1e-05
theta_base = 10000.0
mask_fill = -1e+30

@jax.custom_vjp
def low(v):
    return lax.optimization_barrier(v.astype(jnp.bfloat16)).astype(jnp.float32)

@jax.custom_vjp
def low_back(v):
    return v

def low_keep(v):
    return (low(v), None)

def low_pass(kept, grad):
    return (grad,)

def back_keep(v):
    return (v, None)

def back_low(kept, grad):
    return (low(grad),)
low.defvjp(low_keep, low_pass)
low_back.defvjp(back_keep, back_low)

def matmul(left_side, right_side):
    return jnp.matmul(left_side, right_side, precision=lax.Precision.HIGHEST)

def positions(seq_lens):
    ending = jnp.cumsum(seq_lens, axis=1).astype(jnp.int32)
    places = jnp.arange(SEQ, dtype=jnp.int32)
    passed = places[None, :, None] >= ending[:, None, :]
    segment = lax.optimization_barrier(jnp.sum(passed.astype(jnp.int32), axis=2)).astype(jnp.int32)
    starts = lax.optimization_barrier(jnp.sum(jnp.where(passed, seq_lens[:, None, :], 0), axis=2)).astype(jnp.int32)
    return (segment, places[None, :] - starts)

def rotary(offset):
    half_size = HD // 2
    frequency = theta_base ** (-2.0 * jnp.arange(half_size, dtype=jnp.float32) / HD)
    angles = offset.astype(jnp.float32)[..., None] * frequency
    angles = jnp.concatenate([angles, angles], axis=-1)[:, :, None, :]
    return (jnp.cos(angles), jnp.sin(angles))

def rotate(values, cosine, sines):
    half_size = values.shape[-1] // 2
    rotated = jnp.concatenate([-values[..., half_size:], values[..., :half_size]], axis=-1)
    return values * cosine + rotated * sines

def block_attention(queries, keys, values, segment):
    places = jnp.arange(SEQ, dtype=jnp.int32)
    allowed = (segment[:, None] == segment[None, :]) & (places[None, :] <= places[:, None])
    grouped = queries.reshape(SEQ, KVH, HQ // KVH, HD)
    scores = jnp.einsum('qjgd,kjd->jgqk', grouped, keys, precision=lax.Precision.HIGHEST) * HD ** (-0.5)
    scores = jnp.where(allowed, low_back(scores), mask_fill)
    raised = jnp.exp(scores - lax.optimization_barrier(jnp.max(scores, axis=-1, keepdims=True)))
    weights = raised / lax.optimization_barrier(jnp.sum(raised, axis=-1, keepdims=True))
    output = jnp.einsum('jgqk,kjd->qjgd', low(weights), values, precision=lax.Precision.HIGHEST)
    return output.reshape(SEQ, HQ * HD)

def layer_forward(tokens_in, params, segment, cosine, sines):
    w_query, w_key, w_value, w_out, norm_first, norm_second, w_gate, w_up, w_down = params
    count_blocks = tokens_in.shape[0]
    scale_one = lax.rsqrt(lax.optimization_barrier(jnp.mean(tokens_in * tokens_in, axis=-1, keepdims=True)) + epsilon)
    normed_one = low(tokens_in * scale_one * norm_first)
    queries = low(rotate(low_back(matmul(normed_one, w_query)).reshape(count_blocks, SEQ, HQ, HD), cosine, sines))
    keys = low(rotate(low_back(matmul(normed_one, w_key)).reshape(count_blocks, SEQ, KVH, HD), cosine, sines))
    values = low(low_back(matmul(normed_one, w_value))).reshape(count_blocks, SEQ, KVH, HD)
    checked = jax.checkpoint(block_attention)
    attended = lax.map(lambda entry: checked(entry[0], entry[1], entry[2], entry[3]), (queries, keys, values, segment))
    attended = low(low_back(attended))
    residual = tokens_in + low_back(matmul(attended, w_out))
    scale_two = lax.rsqrt(lax.optimization_barrier(jnp.mean(residual * residual, axis=-1, keepdims=True)) + epsilon)
    normed_two = low(residual * scale_two * norm_second)
    gate_pre = low_back(matmul(normed_two, w_gate))
    up_pre = low_back(matmul(normed_two, w_up))
    hidden = low(jax.nn.silu(gate_pre) * up_pre)
    return residual + low_back(matmul(hidden, w_down))

def reference(tokens, seq_lens, cotangent, w_query, w_key, w_value, w_out, norm_first, norm_second, w_gate, w_up, w_down):
    weights = tuple((w.astype(jnp.float32) for w in (w_query, w_key, w_value, w_out, norm_first, norm_second, w_gate, w_up, w_down)))
    segment, offset = positions(seq_lens)
    cosine, sines = rotary(offset)
    blocks_each = 4 if BLOCKS % 4 == 0 else 1
    rounds = BLOCKS // blocks_each

    def grouped(values):
        return values.reshape((rounds, blocks_each) + values.shape[1:])

    def visit(totals, element):
        values_in, grads_in, seg_part, cos_part, sin_part = element

        def run(inputs, *params):
            return layer_forward(inputs, params, seg_part, cos_part, sin_part)
        result, pull = jax.vjp(run, values_in.astype(jnp.float32), *weights)
        pulled = pull(grads_in.astype(jnp.float32))
        totals = tuple((t + g for t, g in zip(totals, pulled[1:])))
        return (totals, (result.astype(jnp.bfloat16), pulled[0]))
    empty_sums = tuple((jnp.zeros(w.shape, jnp.float32) for w in weights))
    totals, (outputs, grad_inputs) = lax.scan(visit, empty_sums, (grouped(tokens), grouped(cotangent), grouped(segment), grouped(cosine), grouped(sines)))
    return (outputs.reshape(BLOCKS, SEQ, D), grad_inputs.reshape(BLOCKS, SEQ, D), totals[0], totals[1], totals[2], totals[3], totals[4], totals[5], totals[6], totals[7], totals[8])
```

```python
import jax
import jax.numpy as jnp
from jax import lax
from jax.experimental import pallas as pl
from jax.experimental.pallas import tpu as pltpu
from jax.sharding import PartitionSpec as P

HQ = 18
KVH = 6
HD = 64


epsilon = 1e-05
theta_base = 10000.0
mask_fill = -1e30


def contract_rows(left_side, right_side):
    return lax.dot_general(
        left_side, right_side, (((0,), (0,)), ((), ())), preferred_element_type=jnp.float32
    )


def contract_last(left_side, right_side):
    return lax.dot_general(
        left_side, right_side, (((1,), (1,)), ((), ())), preferred_element_type=jnp.float32
    )


def rms_scale(values):
    return lax.rsqrt(jnp.mean(values * values, axis=-1, keepdims=True) + epsilon)


def norm_back(values, inverse_rms, gains, upstream):
    weighted = gains * upstream
    cubed = inverse_rms * inverse_rms * inverse_rms
    return inverse_rms * weighted - values * cubed * jnp.mean(
        values * weighted, axis=-1, keepdims=True
    )


def positions(seq_lens, length):
    ending = jnp.cumsum(seq_lens, axis=1)
    places = jnp.arange(length, dtype=jnp.int32)
    passed = places[None, :, None] >= ending[:, None, :]
    segment = jnp.sum(passed.astype(jnp.int32), axis=2)
    starts = jnp.sum(jnp.where(passed, seq_lens[:, None, :], 0), axis=2)
    return (segment, places[None, :] - starts)


def rotary(offset, head_size):
    half_size = head_size // 2
    frequency = theta_base ** (-2.0 * jnp.arange(half_size, dtype=jnp.float32) / head_size)
    angles = offset.astype(jnp.float32)[..., None] * frequency
    angles = jnp.concatenate([angles, angles], axis=-1)[:, :, None, :]
    return (jnp.cos(angles), jnp.sin(angles))


def rotate(values, cosine, sines):
    half_size = values.shape[-1] // 2
    rotated = jnp.concatenate([-values[..., half_size:], values[..., :half_size]], axis=-1)
    return values * cosine + rotated * sines


def rotate_back(upstream, cosine, sines):
    half_size = upstream.shape[-1] // 2
    scaled = upstream * sines
    return upstream * cosine + jnp.concatenate(
        [scaled[..., half_size:], -scaled[..., :half_size]], axis=-1
    )


def dot_last(left_side, right_side):
    return lax.dot_general(
        left_side, right_side, (((1,), (1,)), ((), ())), preferred_element_type=jnp.float32
    )


def shifted(value, axis, step):
    size = lax.axis_size(axis)
    return lax.ppermute(value, axis, [(i, (i + step) % size) for i in range(size)])


def gather_parts(value, axis):
    return [value] + [shifted(value, axis, step) for step in range(1, lax.axis_size(axis))]


def gather_at(value, axis, place):
    size = lax.axis_size(axis)
    me = lax.axis_index(axis)
    shape = value.shape[:place] + (size,) + value.shape[place:]
    whole = jnp.zeros(shape, value.dtype)
    for step, part in enumerate(gather_parts(value, axis)):
        whole = lax.dynamic_update_slice_in_dim(
            whole, jnp.expand_dims(part, place), (me + size - step) % size, place
        )
    return whole


def scatter_at(value, axis, place):
    size = lax.axis_size(axis)
    me = lax.axis_index(axis)

    def piece(step):
        at = (me + step) % size
        return lax.squeeze(lax.dynamic_slice_in_dim(value, at, 1, place), (place,))

    total = piece(0).astype(jnp.float32)
    for step in range(1, size):
        sent = shifted(piece(step).astype(jnp.bfloat16), axis, step)
        total = total + sent.astype(jnp.float32)
    return total


def gather_two(value, first, second):
    own, width = value.shape
    major = gather_at(value, first, 0)
    both = gather_at(major, second, 1)
    return both.reshape(-1, width)


def scatter_two(value, major, minor):
    rows, width = value.shape
    many, few = lax.axis_size(major), lax.axis_size(minor)
    split = value.reshape(many, few, rows // (many * few), width)
    return scatter_at(scatter_at(split, minor, 1), major, 0)


TILE = 256


def probabilities(query, key, start, first):
    scores = dot_last(query, key)
    rows = lax.broadcasted_iota(jnp.int32, scores.shape, 0) + first
    columns = lax.broadcasted_iota(jnp.int32, scores.shape, 1)
    scores = jnp.where((columns >= start) & (columns <= rows), scores, mask_fill)
    largest = jnp.max(scores, axis=-1, keepdims=True)
    raised = jnp.exp(scores - largest)
    return raised * (1.0 / jnp.sum(raised, axis=-1, keepdims=True))


def attention_kernel(start_ref, query_ref, key_ref, value_ref, out_ref):
    length = query_ref.shape[1]
    tile = min(TILE, length)
    for first in range(0, length, tile):
        last = first + tile
        query = query_ref[0, first:last, :] * jnp.bfloat16(HD**-0.5)
        chances = probabilities(query, key_ref[0, :last, :], start_ref[first:last, :], first)
        out_ref[0, first:last, :] = jnp.dot(
            chances.astype(jnp.bfloat16), value_ref[0, :last, :], preferred_element_type=jnp.float32
        ).astype(jnp.bfloat16)


def attention_back_kernel(
    start_ref, query_ref, key_ref, value_ref, grad_ref, query_grad_ref, key_grad_ref, value_grad_ref
):
    length = query_ref.shape[1]
    tile = min(TILE, length)
    group = HQ // KVH

    @pl.when(pl.program_id(0) % group == 0)
    def _():
        key_grad_ref[...] = jnp.zeros_like(key_grad_ref)
        value_grad_ref[...] = jnp.zeros_like(value_grad_ref)

    for first in range(0, length, tile):
        last = first + tile
        query = query_ref[0, first:last, :] * jnp.bfloat16(HD**-0.5)
        key = key_ref[0, :last, :]
        grad = grad_ref[0, first:last, :]
        chances = probabilities(query, key, start_ref[first:last, :], first)
        chance_grad = dot_last(grad, value_ref[0, :last, :])
        centre = jnp.sum(chances * chance_grad, axis=-1, keepdims=True)
        score_grad = (chances * (chance_grad - centre)).astype(jnp.bfloat16)
        query_grad_ref[0, first:last, :] = jnp.dot(
            score_grad, key, preferred_element_type=jnp.float32
        ) * (HD**-0.5)
        key_grad_ref[0, :last, :] += contract_rows(score_grad, query)
        value_grad_ref[0, :last, :] += contract_rows(chances.astype(jnp.bfloat16), grad)


def attention_specs(length):
    group = HQ // KVH
    start = pl.BlockSpec((length, 1), lambda h: (0, 0))
    query = pl.BlockSpec((1, length, HD), lambda h: (h, 0, 0))
    key = pl.BlockSpec((1, length, HD), lambda h: (h // group, 0, 0))
    return start, query, key


def attention(start, queries, keys, values):
    heads, length, _ = queries.shape
    at_start, at_query, at_key = attention_specs(length)
    pairs = heads * length * length
    return pl.pallas_call(
        attention_kernel,
        grid=(heads,),
        in_specs=[at_start, at_query, at_key, at_key],
        out_specs=at_query,
        out_shape=jax.ShapeDtypeStruct(queries.shape, jnp.bfloat16),
        cost_estimate=pl.CostEstimate(
            flops=30 * pairs * 8, bytes_accessed=heads * length * HD * 8, transcendentals=pairs
        ),
        compiler_params=pltpu.CompilerParams(vmem_limit_bytes=40 * 1024 * 1024),
        name="attention",
    )(start, queries, keys, values)


def attention_back(start, queries, keys, values, grads):
    heads, length, _ = queries.shape
    at_start, at_query, at_key = attention_specs(length)
    pairs = heads * length * length
    return pl.pallas_call(
        attention_back_kernel,
        grid=(heads,),
        in_specs=[at_start, at_query, at_key, at_key, at_query],
        out_specs=[at_query, at_key, at_key],
        out_shape=[
            jax.ShapeDtypeStruct(queries.shape, jnp.float32),
            jax.ShapeDtypeStruct(keys.shape, jnp.float32),
            jax.ShapeDtypeStruct(keys.shape, jnp.float32),
        ],
        cost_estimate=pl.CostEstimate(
            flops=60 * pairs * 16, bytes_accessed=heads * length * HD * 16, transcendentals=pairs
        ),
        compiler_params=pltpu.CompilerParams(vmem_limit_bytes=40 * 1024 * 1024),
        name="attention_back",
    )(start, queries, keys, values, grads)


def local(
    tokens,
    seq_lens,
    cotangent,
    w_query,
    w_key,
    w_value,
    w_out,
    norm_first,
    norm_second,
    w_gate,
    w_up,
    w_down,
):
    blocks, half_len, model_width = tokens.shape
    head_count = lax.axis_size("heads")
    tensor_count = lax.axis_size("tensor")
    length = half_len * head_count
    rows = blocks * length
    heads = w_query.shape[1] // HD
    kv_heads = w_key.shape[1] // HD
    query_width = heads * HD
    key_width = kv_heads * HD
    qkv_width = query_width + 2 * key_width
    inner = w_gate.shape[1]

    own_qkv = jnp.concatenate(
        [w_query, w_key, w_value, norm_first[:, None], norm_second[:, None]], axis=1
    )
    qkv_all = gather_two(own_qkv, "fsdp", "tensor")
    out_t = gather_two(w_out.T, "fsdp", "tensor")
    qkv_w = qkv_all[:, :qkv_width]
    gain_one = qkv_all[:, qkv_width].astype(jnp.float32)
    gain_two = qkv_all[:, qkv_width + 1].astype(jnp.float32)

    rows_one = gather_at(tokens, "heads", 1).reshape(rows, model_width).astype(jnp.float32)
    scale_one = rms_scale(rows_one)
    normed_one = (rows_one * scale_one * gain_one).astype(jnp.bfloat16)
    projected = jnp.dot(normed_one, qkv_w, preferred_element_type=jnp.float32)

    down_grad = cotangent.reshape(blocks * half_len, model_width)
    ffn_own = jnp.concatenate([w_gate, w_up, w_down.T], axis=1)
    projected, down_grad, ffn_own = lax.optimization_barrier((projected, down_grad, ffn_own))
    ffn_w = gather_two(ffn_own, "fsdp", "heads")
    gate_up_w = ffn_w[:, : 2 * inner]
    down_t = ffn_w[:, 2 * inner :]
    grad_parts = gather_parts(down_grad, "tensor")

    segment, offset = positions(seq_lens, length)
    cosine, sines = rotary(offset, HD)
    starts = jnp.arange(length, dtype=jnp.int32)[None, :] - offset

    def to_heads(value, count):
        return value.reshape(blocks, length, count, HD)

    def lead(value):
        return value.transpose(0, 2, 1, 3)

    queries = lead(
        rotate(to_heads(projected[:, :query_width], heads), cosine, sines).astype(jnp.bfloat16)
    )
    keys = lead(
        rotate(
            to_heads(projected[:, query_width : query_width + key_width], kv_heads), cosine, sines
        ).astype(jnp.bfloat16)
    )
    values = lead(
        to_heads(projected[:, query_width + key_width :].astype(jnp.bfloat16), kv_heads)
    )
    attended = jnp.stack(
        [
            attention(starts[b][:, None], queries[b], keys[b], values[b])
            for b in range(blocks)
        ]
    )
    attended_low = attended.transpose(0, 2, 1, 3).reshape(rows, query_width)
    attn_part = dot_last(attended_low, out_t).astype(jnp.bfloat16)
    mixed = scatter_at(
        attn_part.reshape(blocks, head_count, half_len, model_width), "heads", 1
    )
    residual = (tokens.astype(jnp.float32) + mixed).reshape(blocks * half_len, model_width)
    scale_two = rms_scale(residual)
    normed_two = (residual * scale_two * gain_two).astype(jnp.bfloat16)

    ffn_parts = gather_parts(normed_two, "tensor")
    hiddens, gate_ups, grads_back = [], [], []
    for step in range(tensor_count):
        pre = jnp.dot(ffn_parts[step], gate_up_w, preferred_element_type=jnp.float32)
        gate_pre, up_pre = pre[:, :inner], pre[:, inner:]
        sigmoid_gate = jax.nn.sigmoid(gate_pre)
        silu_gate = gate_pre * sigmoid_gate
        hidden_grad = jnp.dot(grad_parts[step], down_t, preferred_element_type=jnp.float32)
        hiddens.append((silu_gate * up_pre).astype(jnp.bfloat16))
        gate_grad = (
            hidden_grad * up_pre * sigmoid_gate * (1.0 + gate_pre * (1.0 - sigmoid_gate))
        ).astype(jnp.bfloat16)
        up_grad = (hidden_grad * silu_gate).astype(jnp.bfloat16)
        gate_ups.append(jnp.concatenate([gate_grad, up_grad], axis=1))
        part = dot_last(gate_ups[step], gate_up_w)
        grads_back.append(
            part if step == 0 else shifted(part.astype(jnp.bfloat16), "tensor", -step)
        )
    normed_grad_two = grads_back[0]
    for part in grads_back[1:]:
        normed_grad_two = normed_grad_two + part.astype(jnp.float32)

    gain_two_part = jnp.sum(normed_grad_two * residual * scale_two, axis=0)
    residual_grad = down_grad.astype(jnp.float32) + norm_back(
        residual, scale_two, gain_two, normed_grad_two
    )
    residual_low = residual_grad.astype(jnp.bfloat16).reshape(blocks, half_len, model_width)
    grad_whole = gather_at(residual_low, "heads", 1).reshape(rows, model_width)

    hiddens[0], grad_whole = lax.optimization_barrier((hiddens[0], grad_whole))
    branch = jnp.zeros((), jnp.float32)
    for step in range(tensor_count):
        part = dot_last(hiddens[step], down_t)
        if step > 0:
            part = shifted(part.astype(jnp.bfloat16), "tensor", -step).astype(jnp.float32)
        branch = branch + part
    layer_out = (residual + branch).reshape(blocks, half_len, model_width).astype(jnp.bfloat16)
    grad_gate_up = contract_rows(jnp.concatenate(ffn_parts), jnp.concatenate(gate_ups))
    grad_down_t = contract_rows(jnp.concatenate(grad_parts), jnp.concatenate(hiddens))
    own_gate_up = scatter_two(grad_gate_up.astype(jnp.bfloat16), "fsdp", "heads")
    own_down = scatter_two(grad_down_t.astype(jnp.bfloat16), "fsdp", "heads")

    attended_grad = jnp.dot(grad_whole, out_t, preferred_element_type=jnp.float32)
    grad_out_t = contract_rows(grad_whole, attended_low)
    own_out = scatter_two(grad_out_t.astype(jnp.bfloat16), "fsdp", "tensor")
    grads = lead(to_heads(attended_grad.astype(jnp.bfloat16), heads))
    backs = [
        attention_back(starts[b][:, None], queries[b], keys[b], values[b], grads[b])
        for b in range(blocks)
    ]
    query_grads, key_grads, value_grads = (
        jnp.stack([back[at] for back in backs]).transpose(0, 2, 1, 3) for at in range(3)
    )
    raw_grad = jnp.concatenate(
        [
            rotate_back(query_grads, cosine, sines).astype(jnp.bfloat16).reshape(rows, query_width),
            rotate_back(key_grads, cosine, sines).astype(jnp.bfloat16).reshape(rows, key_width),
            value_grads.astype(jnp.bfloat16).reshape(rows, key_width),
        ],
        axis=1,
    )
    normed_grad_one = dot_last(raw_grad, qkv_w)
    grad_qkv = contract_rows(normed_one, raw_grad)
    gain_one_part = jnp.sum(normed_grad_one * rows_one * scale_one, axis=0)
    token_part = norm_back(rows_one, scale_one, gain_one, normed_grad_one)
    token_sum = scatter_at(
        token_part.astype(jnp.bfloat16).reshape(blocks, head_count, half_len, model_width),
        "heads",
        1,
    )
    grad_tokens = residual_grad.reshape(blocks, half_len, model_width) + token_sum
    own_qkv_grad = scatter_two(grad_qkv.astype(jnp.bfloat16), "fsdp", "tensor")
    gains = jnp.stack([gain_one_part, gain_two_part], axis=1)
    gains = gains + sum(shifted(gains, "heads", step) for step in range(1, head_count))
    own_gains = scatter_two(gains, "fsdp", "tensor")
    return (
        layer_out,
        grad_tokens,
        own_qkv_grad[:, :query_width],
        own_qkv_grad[:, query_width : query_width + key_width],
        own_qkv_grad[:, query_width + key_width :],
        own_out.T,
        own_gains[:, 0],
        own_gains[:, 1],
        own_gate_up[:, :inner],
        own_gate_up[:, inner:],
        own_down.T,
    )


def solution(mesh):
    placed = (
        P(("fsdp", "tensor"), "heads", None),
        P(("fsdp", "tensor"), None),
        P(("fsdp", "tensor"), "heads", None),
        P(("fsdp", "tensor"), "heads"),
        P(("fsdp", "tensor"), "heads"),
        P(("fsdp", "tensor"), "heads"),
        P("heads", ("fsdp", "tensor")),
        P(("fsdp", "tensor")),
        P(("fsdp", "tensor")),
        P(("fsdp", "heads"), "tensor"),
        P(("fsdp", "heads"), "tensor"),
        P("tensor", ("fsdp", "heads")),
    )
    return jax.shard_map(
        local,
        mesh=mesh,
        in_specs=placed,
        out_specs=(
            P(("fsdp", "tensor"), "heads", None),
            P(("fsdp", "tensor"), "heads", None),
            P(("fsdp", "tensor"), "heads"),
            P(("fsdp", "tensor"), "heads"),
            P(("fsdp", "tensor"), "heads"),
            P("heads", ("fsdp", "tensor")),
            P(("fsdp", "tensor")),
            P(("fsdp", "tensor")),
            P(("fsdp", "heads"), "tensor"),
            P(("fsdp", "heads"), "tensor"),
            P("tensor", ("fsdp", "heads")),
        ),
        check_vma=False,
    )
```

```python
import jax
import jax.numpy as jnp
from jax import lax
from jax.experimental import pallas as pl
from jax.experimental.pallas import tpu as pltpu
from jax.sharding import PartitionSpec as P

HQ = 18
KVH = 6
HD = 64


epsilon = 1e-05
theta_base = 10000.0
mask_fill = -1e30


def contract_rows(left_side, right_side):
    return lax.dot_general(
        left_side, right_side, (((0,), (0,)), ((), ())), preferred_element_type=jnp.float32
    )


def contract_last(left_side, right_side):
    return lax.dot_general(
        left_side, right_side, (((1,), (1,)), ((), ())), preferred_element_type=jnp.float32
    )


def rms_scale(values):
    return lax.rsqrt(jnp.mean(values * values, axis=-1, keepdims=True) + epsilon)


def norm_back(values, inverse_rms, gains, upstream):
    weighted = gains * upstream
    cubed = inverse_rms * inverse_rms * inverse_rms
    return inverse_rms * weighted - values * cubed * jnp.mean(
        values * weighted, axis=-1, keepdims=True
    )


def positions(seq_lens, length):
    ending = jnp.cumsum(seq_lens, axis=1)
    places = jnp.arange(length, dtype=jnp.int32)
    passed = places[None, :, None] >= ending[:, None, :]
    segment = jnp.sum(passed.astype(jnp.int32), axis=2)
    starts = jnp.sum(jnp.where(passed, seq_lens[:, None, :], 0), axis=2)
    return (segment, places[None, :] - starts)


def rotary(offset, head_size):
    half_size = head_size // 2
    frequency = theta_base ** (-2.0 * jnp.arange(half_size, dtype=jnp.float32) / head_size)
    angles = offset.astype(jnp.float32)[..., None] * frequency
    angles = jnp.concatenate([angles, angles], axis=-1)[:, :, None, :]
    return (jnp.cos(angles), jnp.sin(angles))


def rotate(values, cosine, sines):
    half_size = values.shape[-1] // 2
    rotated = jnp.concatenate([-values[..., half_size:], values[..., :half_size]], axis=-1)
    return values * cosine + rotated * sines


def rotate_back(upstream, cosine, sines):
    half_size = upstream.shape[-1] // 2
    scaled = upstream * sines
    return upstream * cosine + jnp.concatenate(
        [scaled[..., half_size:], -scaled[..., :half_size]], axis=-1
    )


def dot_last(left_side, right_side):
    return lax.dot_general(
        left_side, right_side, (((1,), (1,)), ((), ())), preferred_element_type=jnp.float32
    )


def shifted(value, axis, step):
    size = lax.axis_size(axis)
    return lax.ppermute(value, axis, [(i, (i + step) % size) for i in range(size)])


def gather_parts(value, axis):
    return [value] + [shifted(value, axis, step) for step in range(1, lax.axis_size(axis))]


def gather_at(value, axis, place):
    size = lax.axis_size(axis)
    me = lax.axis_index(axis)
    shape = value.shape[:place] + (size,) + value.shape[place:]
    whole = jnp.zeros(shape, value.dtype)
    for step, part in enumerate(gather_parts(value, axis)):
        whole = lax.dynamic_update_slice_in_dim(
            whole, jnp.expand_dims(part, place), (me + size - step) % size, place
        )
    return whole


def scatter_at(value, axis, place):
    size = lax.axis_size(axis)
    me = lax.axis_index(axis)

    def piece(step):
        at = (me + step) % size
        return lax.squeeze(lax.dynamic_slice_in_dim(value, at, 1, place), (place,))

    total = piece(0).astype(jnp.float32)
    for step in range(1, size):
        sent = shifted(piece(step).astype(jnp.bfloat16), axis, step)
        total = total + sent.astype(jnp.float32)
    return total


def gather_two(value, first, second):
    own, width = value.shape
    major = gather_at(value, first, 0)
    both = gather_at(major, second, 1)
    return both.reshape(-1, width)


def scatter_two(value, major, minor):
    rows, width = value.shape
    many, few = lax.axis_size(major), lax.axis_size(minor)
    split = value.reshape(many, few, rows // (many * few), width)
    return scatter_at(scatter_at(split, minor, 1), major, 0)


TILE = 256


def probabilities(query, key, start, first):
    scores = dot_last(query, key)
    rows = lax.broadcasted_iota(jnp.int32, scores.shape, 0) + first
    columns = lax.broadcasted_iota(jnp.int32, scores.shape, 1)
    scores = jnp.where((columns >= start) & (columns <= rows), scores, mask_fill)
    largest = jnp.max(scores, axis=-1, keepdims=True)
    raised = jnp.exp(scores - largest)
    return raised * (1.0 / jnp.sum(raised, axis=-1, keepdims=True))


def attention_kernel(start_ref, query_ref, key_ref, value_ref, out_ref):
    length = query_ref.shape[1]
    tile = min(TILE, length)
    for first in range(0, length, tile):
        last = first + tile
        query = query_ref[0, first:last, :] * jnp.bfloat16(HD**-0.5)
        chances = probabilities(query, key_ref[0, :last, :], start_ref[first:last, :], first)
        out_ref[0, first:last, :] = jnp.dot(
            chances.astype(jnp.bfloat16), value_ref[0, :last, :], preferred_element_type=jnp.float32
        ).astype(jnp.bfloat16)


def attention_back_kernel(
    start_ref, query_ref, key_ref, value_ref, grad_ref, query_grad_ref, key_grad_ref, value_grad_ref
):
    length = query_ref.shape[1]
    tile = min(TILE, length)
    group = HQ // KVH

    @pl.when(pl.program_id(0) % group == 0)
    def _():
        key_grad_ref[...] = jnp.zeros_like(key_grad_ref)
        value_grad_ref[...] = jnp.zeros_like(value_grad_ref)

    for first in range(0, length, tile):
        last = first + tile
        query = query_ref[0, first:last, :] * jnp.bfloat16(HD**-0.5)
        key = key_ref[0, :last, :]
        grad = grad_ref[0, first:last, :]
        chances = probabilities(query, key, start_ref[first:last, :], first)
        chance_grad = dot_last(grad, value_ref[0, :last, :])
        centre = jnp.sum(chances * chance_grad, axis=-1, keepdims=True)
        score_grad = (chances * (chance_grad - centre)).astype(jnp.bfloat16)
        query_grad_ref[0, first:last, :] = jnp.dot(
            score_grad, key, preferred_element_type=jnp.float32
        ) * (HD**-0.5)
        key_grad_ref[0, :last, :] += contract_rows(score_grad, query)
        value_grad_ref[0, :last, :] += contract_rows(chances.astype(jnp.bfloat16), grad)


def attention_specs(length):
    group = HQ // KVH
    start = pl.BlockSpec((length, 1), lambda h: (0, 0))
    query = pl.BlockSpec((1, length, HD), lambda h: (h, 0, 0))
    key = pl.BlockSpec((1, length, HD), lambda h: (h // group, 0, 0))
    return start, query, key


def attention(start, queries, keys, values):
    heads, length, _ = queries.shape
    at_start, at_query, at_key = attention_specs(length)
    pairs = heads * length * length
    return pl.pallas_call(
        attention_kernel,
        grid=(heads,),
        in_specs=[at_start, at_query, at_key, at_key],
        out_specs=at_query,
        out_shape=jax.ShapeDtypeStruct(queries.shape, jnp.bfloat16),
        cost_estimate=pl.CostEstimate(
            flops=30 * pairs * 8, bytes_accessed=heads * length * HD * 8, transcendentals=pairs
        ),
        compiler_params=pltpu.CompilerParams(vmem_limit_bytes=40 * 1024 * 1024),
        name="attention",
    )(start, queries, keys, values)


def attention_back(start, queries, keys, values, grads):
    heads, length, _ = queries.shape
    at_start, at_query, at_key = attention_specs(length)
    pairs = heads * length * length
    return pl.pallas_call(
        attention_back_kernel,
        grid=(heads,),
        in_specs=[at_start, at_query, at_key, at_key, at_query],
        out_specs=[at_query, at_key, at_key],
        out_shape=[
            jax.ShapeDtypeStruct(queries.shape, jnp.float32),
            jax.ShapeDtypeStruct(keys.shape, jnp.float32),
            jax.ShapeDtypeStruct(keys.shape, jnp.float32),
        ],
        cost_estimate=pl.CostEstimate(
            flops=60 * pairs * 16, bytes_accessed=heads * length * HD * 16, transcendentals=pairs
        ),
        compiler_params=pltpu.CompilerParams(vmem_limit_bytes=40 * 1024 * 1024),
        name="attention_back",
    )(start, queries, keys, values, grads)


def local(
    tokens,
    seq_lens,
    cotangent,
    w_query,
    w_key,
    w_value,
    w_out,
    norm_first,
    norm_second,
    w_gate,
    w_up,
    w_down,
):
    blocks, half_len, model_width = tokens.shape
    head_count = lax.axis_size("heads")
    tensor_count = lax.axis_size("tensor")
    length = half_len * head_count
    rows = blocks * length
    heads = w_query.shape[1] // HD
    kv_heads = w_key.shape[1] // HD
    query_width = heads * HD
    key_width = kv_heads * HD
    qkv_width = query_width + 2 * key_width
    inner = w_gate.shape[1]

    own_qkv = jnp.concatenate(
        [w_query, w_key, w_value, norm_first[:, None], norm_second[:, None]], axis=1
    )
    ffn_own = jnp.concatenate([w_gate, w_up, w_down.T], axis=1)
    qkv_major = gather_at(own_qkv, "fsdp", 0)
    qkv_major, ffn_own = lax.optimization_barrier((qkv_major, ffn_own))
    qkv_all = gather_at(qkv_major, "tensor", 1).reshape(model_width, -1)
    out_t = gather_two(w_out.T, "fsdp", "tensor")
    down_grad = cotangent.reshape(blocks * half_len, model_width)
    qkv_all, down_grad = lax.optimization_barrier((qkv_all, down_grad))
    qkv_w = qkv_all[:, :qkv_width]
    gain_one = qkv_all[:, qkv_width].astype(jnp.float32)
    gain_two = qkv_all[:, qkv_width + 1].astype(jnp.float32)

    rows_one = gather_at(tokens, "heads", 1).reshape(rows, model_width).astype(jnp.float32)
    scale_one = rms_scale(rows_one)
    normed_one = (rows_one * scale_one * gain_one).astype(jnp.bfloat16)
    projected = jnp.dot(normed_one, qkv_w, preferred_element_type=jnp.float32)

    ffn_w = gather_two(ffn_own, "fsdp", "heads")
    gate_up_w = ffn_w[:, : 2 * inner]
    down_t = ffn_w[:, 2 * inner :]
    grad_parts = gather_parts(down_grad, "tensor")

    segment, offset = positions(seq_lens, length)
    cosine, sines = rotary(offset, HD)
    starts = jnp.arange(length, dtype=jnp.int32)[None, :] - offset

    def to_heads(value, count):
        return value.reshape(blocks, length, count, HD)

    def lead(value):
        return value.transpose(0, 2, 1, 3)

    queries = lead(
        rotate(to_heads(projected[:, :query_width], heads), cosine, sines).astype(jnp.bfloat16)
    )
    keys = lead(
        rotate(
            to_heads(projected[:, query_width : query_width + key_width], kv_heads), cosine, sines
        ).astype(jnp.bfloat16)
    )
    values = lead(
        to_heads(projected[:, query_width + key_width :].astype(jnp.bfloat16), kv_heads)
    )
    attended = jnp.stack(
        [
            attention(starts[b][:, None], queries[b], keys[b], values[b])
            for b in range(blocks)
        ]
    )
    attended_low = attended.transpose(0, 2, 1, 3).reshape(rows, query_width)
    attn_part = dot_last(attended_low, out_t).astype(jnp.bfloat16)
    mixed = scatter_at(
        attn_part.reshape(blocks, head_count, half_len, model_width), "heads", 1
    )
    residual = (tokens.astype(jnp.float32) + mixed).reshape(blocks * half_len, model_width)
    scale_two = rms_scale(residual)
    normed_two = (residual * scale_two * gain_two).astype(jnp.bfloat16)

    ffn_parts = gather_parts(normed_two, "tensor")
    hiddens, gate_ups, grads_back = [], [], []
    for step in range(tensor_count):
        pre = jnp.dot(ffn_parts[step], gate_up_w, preferred_element_type=jnp.float32)
        gate_pre, up_pre = pre[:, :inner], pre[:, inner:]
        sigmoid_gate = jax.nn.sigmoid(gate_pre)
        silu_gate = gate_pre * sigmoid_gate
        hidden_grad = jnp.dot(grad_parts[step], down_t, preferred_element_type=jnp.float32)
        hiddens.append((silu_gate * up_pre).astype(jnp.bfloat16))
        gate_grad = (
            hidden_grad * up_pre * sigmoid_gate * (1.0 + gate_pre * (1.0 - sigmoid_gate))
        ).astype(jnp.bfloat16)
        up_grad = (hidden_grad * silu_gate).astype(jnp.bfloat16)
        gate_ups.append(jnp.concatenate([gate_grad, up_grad], axis=1))
        part = dot_last(gate_ups[step], gate_up_w)
        grads_back.append(
            part if step == 0 else shifted(part.astype(jnp.bfloat16), "tensor", -step)
        )
    normed_grad_two = grads_back[0]
    for part in grads_back[1:]:
        normed_grad_two = normed_grad_two + part.astype(jnp.float32)

    gain_two_part = jnp.sum(normed_grad_two * residual * scale_two, axis=0)
    residual_grad = down_grad.astype(jnp.float32) + norm_back(
        residual, scale_two, gain_two, normed_grad_two
    )
    residual_low = residual_grad.astype(jnp.bfloat16).reshape(blocks, half_len, model_width)
    grad_whole = gather_at(residual_low, "heads", 1).reshape(rows, model_width)

    hiddens[0], grad_whole = lax.optimization_barrier((hiddens[0], grad_whole))
    branch = jnp.zeros((), jnp.float32)
    for step in range(tensor_count):
        part = dot_last(hiddens[step], down_t)
        if step > 0:
            part = shifted(part.astype(jnp.bfloat16), "tensor", -step).astype(jnp.float32)
        branch = branch + part
    layer_out = (residual + branch).reshape(blocks, half_len, model_width).astype(jnp.bfloat16)
    grad_gate_up = contract_rows(jnp.concatenate(ffn_parts), jnp.concatenate(gate_ups))
    grad_down_t = contract_rows(jnp.concatenate(grad_parts), jnp.concatenate(hiddens))
    own_gate_up = scatter_two(grad_gate_up.astype(jnp.bfloat16), "fsdp", "heads")
    own_down = scatter_two(grad_down_t.astype(jnp.bfloat16), "fsdp", "heads")

    attended_grad = jnp.dot(grad_whole, out_t, preferred_element_type=jnp.float32)
    grad_out_t = contract_rows(grad_whole, attended_low)
    own_out = scatter_two(grad_out_t.astype(jnp.bfloat16), "fsdp", "tensor")
    grads = lead(to_heads(attended_grad.astype(jnp.bfloat16), heads))
    backs = [
        attention_back(starts[b][:, None], queries[b], keys[b], values[b], grads[b])
        for b in range(blocks)
    ]
    query_grads, key_grads, value_grads = (
        jnp.stack([back[at] for back in backs]).transpose(0, 2, 1, 3) for at in range(3)
    )
    raw_grad = jnp.concatenate(
        [
            rotate_back(query_grads, cosine, sines).astype(jnp.bfloat16).reshape(rows, query_width),
            rotate_back(key_grads, cosine, sines).astype(jnp.bfloat16).reshape(rows, key_width),
            value_grads.astype(jnp.bfloat16).reshape(rows, key_width),
        ],
        axis=1,
    )
    normed_grad_one = dot_last(raw_grad, qkv_w)
    grad_qkv = contract_rows(normed_one, raw_grad)
    gain_one_part = jnp.sum(normed_grad_one * rows_one * scale_one, axis=0)
    token_part = norm_back(rows_one, scale_one, gain_one, normed_grad_one)
    token_sum = scatter_at(
        token_part.astype(jnp.bfloat16).reshape(blocks, head_count, half_len, model_width),
        "heads",
        1,
    )
    grad_tokens = residual_grad.reshape(blocks, half_len, model_width) + token_sum
    own_qkv_grad = scatter_two(grad_qkv.astype(jnp.bfloat16), "fsdp", "tensor")
    gains = jnp.stack([gain_one_part, gain_two_part], axis=1)
    gains = gains + sum(shifted(gains, "heads", step) for step in range(1, head_count))
    own_gains = scatter_two(gains, "fsdp", "tensor")
    return (
        layer_out,
        grad_tokens,
        own_qkv_grad[:, :query_width],
        own_qkv_grad[:, query_width : query_width + key_width],
        own_qkv_grad[:, query_width + key_width :],
        own_out.T,
        own_gains[:, 0],
        own_gains[:, 1],
        own_gate_up[:, :inner],
        own_gate_up[:, inner:],
        own_down.T,
    )


def solution(mesh):
    placed = (
        P(("fsdp", "tensor"), "heads", None),
        P(("fsdp", "tensor"), None),
        P(("fsdp", "tensor"), "heads", None),
        P(("fsdp", "tensor"), "heads"),
        P(("fsdp", "tensor"), "heads"),
        P(("fsdp", "tensor"), "heads"),
        P("heads", ("fsdp", "tensor")),
        P(("fsdp", "tensor")),
        P(("fsdp", "tensor")),
        P(("fsdp", "heads"), "tensor"),
        P(("fsdp", "heads"), "tensor"),
        P("tensor", ("fsdp", "heads")),
    )
    return jax.shard_map(
        local,
        mesh=mesh,
        in_specs=placed,
        out_specs=(
            P(("fsdp", "tensor"), "heads", None),
            P(("fsdp", "tensor"), "heads", None),
            P(("fsdp", "tensor"), "heads"),
            P(("fsdp", "tensor"), "heads"),
            P(("fsdp", "tensor"), "heads"),
            P("heads", ("fsdp", "tensor")),
            P(("fsdp", "tensor")),
            P(("fsdp", "tensor")),
            P(("fsdp", "heads"), "tensor"),
            P(("fsdp", "heads"), "tensor"),
            P("tensor", ("fsdp", "heads")),
        ),
        check_vma=False,
    )
```
